32 devices in a mesh: grp: 2 (over y), par: 8 (over z, x), smp: 2 (over core).
Axes of the slice: x: 2, y: 2, z: 4, core: 2. Of those that a mesh axis runs over, the one named last changes fastest.
Arguments:
- log_derivs: bfloat16 [2048, 524288], P(('grp', 'smp'), 'par'), parts along dimension 0, may hold values from -2000 to 2000, as said below
- spin_states: int32 [2048, 100], P(('grp', 'smp')), parts along dimension 0, may hold values from 0 to 1
- offdiag_energy: float32 [2048], P(('grp', 'smp')), parts along dimension 0, may hold values from -24 to 24
Outputs:
- param_update: float32 [1048576], P(('grp', 'par', 'smp')), parts along dimension 0
- coefficients: float32 [2048], P('grp'), parts along dimension 0
The draws below stay inside these ranges and needn't reach their ends.
There are 2 independent parts, one for each index of `grp`. The reference program is written for one: setup_inputs(seed, part) draws one part's arguments, and reference() takes and returns one part's arrays. A program takes and returns all parts, laid end to end along the dimension named above; each array names one. Nothing has to cross between parts.
Inputs may be any that keep to these rules, and one draw needn't show every extreme that they name: `log_derivs`: real values.
All inputs are finite; a program needn't handle non-finite values.
Results may differ from the reference program's by a relative error of at most 0.0031.
Values may be sent and summed in bfloat16 or wider, within the bound.
A program may use at most 512 MiB of HBM per device.

```python
import math
import jax
import jax.numpy as jnp
from jax import lax

NP = 524288
SIDE = 10
SITES = 100
NS = 1024


def draw_log_derivs(key, part):
    subkeys = jax.random.split(key, 6)
    factor_count = 384
    rough = jax.random.truncated_normal(subkeys[0], -5.0, 5.0, (NS, NP), jnp.float32)
    row_scale = jnp.exp(jax.random.uniform(subkeys[1], (NS, 1), jnp.float32, 0.0, 0.5 * math.log(10.0)))
    loads = jax.random.truncated_normal(subkeys[3], -5.0, 5.0, (NS, factor_count), jnp.float32)
    share = 3.0
    offset = 2.0
    ratio = math.exp(-math.log(1000.0) / factor_count)
    total_variance = (1.0 - ratio ** factor_count) / (1.0 - ratio)
    decay = jnp.exp(jnp.arange(factor_count, dtype=jnp.float32) * (-0.5 * math.log(1000.0) / factor_count))
    factor_scale = decay * math.sqrt(share / total_variance)
    spread = jnp.exp(jax.random.uniform(subkeys[2], (1, NP), jnp.float32, 0.0, math.log(3.0)))
    ramp = jnp.exp(jnp.arange(NP, dtype=jnp.float32)[None, :] * (math.log(3.0) / NP)) / 3.0
    basis = jax.random.truncated_normal(subkeys[4], -5.0, 5.0, (factor_count, NP), jnp.float32)
    summed = 0.3 * rough + jnp.dot(loads * factor_scale[None, :], basis, precision=lax.Precision.HIGHEST, preferred_element_type=jnp.float32)
    centre = offset * jax.random.truncated_normal(subkeys[5], -5.0, 5.0, (1, NP), jnp.float32)
    return jnp.clip(row_scale * (spread * ramp) * summed + centre, -1999.0, 1999.0).astype(jnp.bfloat16)


def place_ends(entries, rng, low, largest):
    shape = entries.shape
    place = [jax.random.randint(jax.random.fold_in(rng, axis), (), 0, shape[axis]) for axis in range(len(shape))]
    entries = entries.at[tuple(place)].set(low)
    longest = shape.index(max(shape))
    place[longest] = (place[longest] + 1) % shape[longest]
    return entries.at[tuple(place)].set(largest)


def level_of(rng, shape, pieces, low, high):
    def one(dim, parts):
        steps = jax.random.uniform(jax.random.fold_in(jax.random.fold_in(rng, 6), dim), (parts,), jnp.float32, low / len(pieces), high / len(pieces))
        return jnp.repeat(jnp.exp(steps), shape[dim] // parts).reshape((-1,) + (1,) * (len(shape) - dim - 1))

    level = one(*pieces[0])
    for cut in pieces[1:]:
        level = level * one(*cut)
    return level


def gaussian(rng, shape, scale, limit, pieces=(), kind=jnp.bfloat16):
    factor_of = level_of(rng, shape, pieces, -0.22, 0.18) if pieces else 1.0
    drawn = jax.random.normal(rng, shape, jnp.float32) * scale * factor_of
    return jnp.minimum(jnp.maximum(drawn, -limit), limit).astype(kind)


def setup_inputs(seed: int = 0, part: int = 0) -> dict:
    keys = jax.random.split(jax.random.key(seed), 4)
    part_splits = jax.random.split(jax.random.fold_in(keys[3], part), 4)
    log_derivs = draw_log_derivs(jax.random.fold_in(jax.random.fold_in(keys[3], part), 71), part)
    spin_states = place_ends(jax.random.randint(part_splits[1], (NS, SITES), 0, 2), jax.random.fold_in(part_splits[1], 1), 0, 1).astype(jnp.int32)
    offdiag_energy = gaussian(part_splits[2], (NS,), 4.0, 24.0, ((0, 2),), jnp.float32)
    return dict(log_derivs=log_derivs, spin_states=spin_states, offdiag_energy=offdiag_energy)


near_coupling = 1.0
diagonal_coupling = 0.5
damp_ratio = 0.05

def lattice_energy(spin_states):
    signs = (2 * spin_states - 1).astype(jnp.float32).reshape(spin_states.shape[0], SIDE, SIDE)
    nearest = signs * jnp.roll(signs, -1, 1) + signs * jnp.roll(signs, -1, 2)
    shifted = jnp.roll(signs, -1, 1)
    diagonal_pairs = signs * jnp.roll(shifted, -1, 2) + signs * jnp.roll(shifted, 1, 2)
    return near_coupling * lax.optimization_barrier(jnp.sum(nearest, axis=(1, 2))) + diagonal_coupling * lax.optimization_barrier(jnp.sum(diagonal_pairs, axis=(1, 2)))

def reference(log_derivs, spin_states, offdiag_energy):
    energies = lattice_energy(spin_states) + offdiag_energy
    centred_energy = energies - jnp.mean(energies)
    col_means = lax.optimization_barrier(jnp.mean(log_derivs.astype(jnp.float32), axis=0))
    centred = (log_derivs.astype(jnp.float32) - col_means[None, :]).astype(jnp.bfloat16)
    gram_matrix = lax.dot_general(centred.astype(jnp.float32), centred.astype(jnp.float32), (((1,), (1,)), ((), ())), preferred_element_type=jnp.float32) / NP
    damping = damp_ratio * jnp.trace(gram_matrix) / NS
    system = gram_matrix + damping * jnp.eye(NS, dtype=jnp.float32)
    factor = jnp.linalg.cholesky(system)
    coefficients = jax.scipy.linalg.cho_solve((factor, True), centred_energy)
    param_update = -jnp.dot(coefficients.astype(jnp.float32), centred.astype(jnp.float32), precision=lax.Precision.HIGHEST, preferred_element_type=jnp.float32) / math.sqrt(NS)
    return (param_update, coefficients)
```

```python
import functools
import math

import jax
import jax.numpy as jnp
from jax import lax
from jax.experimental import pallas as pl
from jax.experimental.pallas import tpu as pltpu
from jax.sharding import PartitionSpec as P

NP = 524288
SIDE = 10


near_coupling = 1.0
diagonal_coupling = 0.5
damp_ratio = 0.05


def lattice_energy(spin_states):
    signs = (2 * spin_states - 1).astype(jnp.float32).reshape(spin_states.shape[0], SIDE, SIDE)
    nearest = signs * jnp.roll(signs, -1, 1) + signs * jnp.roll(signs, -1, 2)
    shifted = jnp.roll(signs, -1, 1)
    diagonal_pairs = signs * jnp.roll(shifted, -1, 2) + signs * jnp.roll(shifted, 1, 2)
    return near_coupling * jnp.sum(nearest, axis=(1, 2)) + diagonal_coupling * jnp.sum(
        diagonal_pairs, axis=(1, 2)
    )


HI = lax.Precision.HIGHEST
BLK = 128


def dot_f32(left, right, dims):
    return lax.dot_general(
        left, right, (dims, ((), ())), precision=HI, preferred_element_type=jnp.float32
    )


def factor_diagonal(work, inv_root):
    sub = lax.broadcasted_iota(jnp.int32, (8, BLK), 0)
    lane = lax.broadcasted_iota(jnp.int32, (8, BLK), 1)
    for r in range(0, BLK, 8):
        rows = work[r : r + 8, :]
        upper, side = rows[:, :BLK], rows[:, BLK:]
        cols = [jnp.broadcast_to(upper[:, r + j : r + j + 1], (8, BLK)) for j in range(8)]
        pivots = jnp.ones((8, BLK), jnp.float32)
        for j in range(8):
            recip = 1.0 / jnp.broadcast_to(cols[j][j : j + 1, :], (8, BLK))
            pivots = jnp.where(sub == j, recip, pivots)
            if j == 7:
                break
            ratio = jnp.where(sub > j, cols[j] * recip, 0.0)
            for l in range(j + 1, 8):
                cols[l] = cols[l] - ratio * cols[l][j : j + 1, :]
            upper = upper - ratio * upper[j : j + 1, :]
            side = side - ratio * side[j : j + 1, :]
        inv_root[r : r + 8, :] = side * jnp.sqrt(pivots)
        if r + 8 < BLK:
            scaled = jnp.where(lane >= r + 8, upper * pivots, 0.0)
            change = dot_f32(scaled, jnp.concatenate([upper, side], axis=1), ((0,), (0,)))
            work[r + 8 :, :] = work[r + 8 :, :] - change[r + 8 :, :]


def solve_kernel(gram_ref, energy_ref, out_ref, a, work, inv_roots):
    order = gram_ref.shape[0]
    blocks = order // BLK
    eye = jnp.where(
        lax.broadcasted_iota(jnp.int32, (BLK, BLK), 0)
        == lax.broadcasted_iota(jnp.int32, (BLK, BLK), 1),
        1.0,
        0.0,
    )
    diag = jnp.zeros((BLK, BLK), jnp.float32)
    for k in range(blocks):
        s = slice(k * BLK, (k + 1) * BLK)
        diag = diag + eye * gram_ref[s, s]
    damping = damp_ratio * (jnp.sum(diag) / order)
    a[...] = gram_ref[...]
    rhs = energy_ref[...]
    rhs = rhs - jnp.sum(rhs, axis=1, keepdims=True) / order
    solved = []
    for k in range(blocks):
        s = slice(k * BLK, (k + 1) * BLK)
        work[:, :BLK] = a[s, s] + damping * eye
        work[:, BLK:] = eye
        factor_diagonal(work, inv_roots.at[k])
        inv_root = inv_roots[k]
        y = dot_f32(rhs[:, :BLK], inv_root, ((1,), (1,)))
        solved.append(y)
        if k + 1 < blocks:
            panel = dot_f32(a[(k + 1) * BLK :, s], inv_root, ((1,), (1,)))
            a[(k + 1) * BLK :, s] = panel
            rhs = rhs[:, BLK:] - dot_f32(y, panel, ((1,), (1,)))
            for c in range(k + 1, blocks):
                t = slice(c * BLK, (c + 1) * BLK)
                a[c * BLK :, t] = a[c * BLK :, t] - dot_f32(
                    panel[(c - k - 1) * BLK :], panel[(c - k - 1) * BLK : (c - k) * BLK], ((1,), (1,))
                )
    below = None
    for k in reversed(range(blocks)):
        z = solved[k]
        if below is not None:
            z = z - dot_f32(below, a[(k + 1) * BLK :, k * BLK : (k + 1) * BLK], ((1,), (0,)))
        x = dot_f32(z, inv_roots[k], ((1,), (0,)))
        below = x if below is None else jnp.concatenate([x, below], axis=1)
    out_ref[...] = below


def solve_system(gram_matrix, energies):
    order = gram_matrix.shape[0]
    rows = jnp.broadcast_to(energies[None, :], (8, order))
    out = pl.pallas_call(
        solve_kernel,
        out_shape=jax.ShapeDtypeStruct((8, order), jnp.float32),
        in_specs=[pl.BlockSpec(memory_space=pltpu.VMEM)] * 2,
        out_specs=pl.BlockSpec(memory_space=pltpu.VMEM),
        scratch_shapes=[
            pltpu.VMEM((order, order), jnp.float32),
            pltpu.VMEM((BLK, 2 * BLK), jnp.float32),
            pltpu.VMEM((order // BLK, BLK, BLK), jnp.float32),
        ],
        compiler_params=pltpu.CompilerParams(vmem_limit_bytes=40 * 2**20),
        name="solve",
    )(gram_matrix, rows)
    return out[0]


def local(log_derivs, spin_states, offdiag_energy):
    row_count, width = log_derivs.shape
    cores = lax.axis_size("smp")
    total_rows = row_count * cores
    part = width // cores
    me = lax.axis_index("smp")
    local_energy = lattice_energy(spin_states) + offdiag_energy
    energies = lax.all_gather(local_energy, "smp", axis=0, tiled=True)
    own = lax.dynamic_slice_in_dim(log_derivs, me * part, part, 1)
    theirs = lax.dynamic_slice_in_dim(log_derivs, (1 - me) * part, part, 1)
    got = lax.ppermute(theirs, "smp", [(0, 1), (1, 0)])
    first = jnp.where(me == 0, own, got)
    second = jnp.where(me == 0, got, own)
    rows = jnp.concatenate([first, second], axis=0)
    means = jnp.sum(rows.astype(jnp.float32), axis=0) / total_rows
    centred = (rows.astype(jnp.float32) - means[None, :]).astype(jnp.bfloat16)
    partial_gram = lax.dot_general(
        centred, centred, (((1,), (1,)), ((), ())), preferred_element_type=jnp.float32
    )
    gram_matrix = lax.psum(partial_gram, ("par", "smp")) / NP
    coefficients = solve_system(gram_matrix, energies)
    param_update = -jnp.dot(
        coefficients,
        centred.astype(jnp.float32),
        precision=lax.Precision.HIGHEST,
        preferred_element_type=jnp.float32,
    ) / math.sqrt(total_rows)
    return (param_update, coefficients)


def solution(mesh):
    placed = (P(("grp", "smp"), "par"), P(("grp", "smp"), None), P(("grp", "smp")))
    return jax.shard_map(
        local,
        mesh=mesh,
        in_specs=placed,
        out_specs=(P(("grp", "par", "smp")), P("grp")),
        check_vma=False,
    )
```

```python
import functools
import math

import jax
import jax.numpy as jnp
from jax import lax
from jax.experimental import pallas as pl
from jax.experimental.pallas import tpu as pltpu
from jax.sharding import PartitionSpec as P

NP = 524288
SIDE = 10


near_coupling = 1.0
diagonal_coupling = 0.5
damp_ratio = 0.05


def lattice_energy(spin_states):
    signs = (2 * spin_states - 1).astype(jnp.float32).reshape(spin_states.shape[0], SIDE, SIDE)
    nearest = signs * jnp.roll(signs, -1, 1) + signs * jnp.roll(signs, -1, 2)
    shifted = jnp.roll(signs, -1, 1)
    diagonal_pairs = signs * jnp.roll(shifted, -1, 2) + signs * jnp.roll(shifted, 1, 2)
    return near_coupling * jnp.sum(nearest, axis=(1, 2)) + diagonal_coupling * jnp.sum(
        diagonal_pairs, axis=(1, 2)
    )


TILE = 256
WIDE = 2048
SUB = 512


def block_pairs(order):
    return [(i, j) for i in range(order // TILE) for j in range(i + 1)]


def gram_kernel(me_ref, own_ref, got_ref, start_ref, centred_ref, gram_ref):
    rows = own_ref.shape[0]
    me = me_ref[0]
    own_at = pl.ds(pl.multiple_of(me * rows, rows), rows)
    got_at = pl.ds(pl.multiple_of((1 - me) * rows, rows), rows)

    @pl.when(pl.program_id(0) == 0)
    def _():
        gram_ref[...] = start_ref[...]

    def centre(n):
        at = slice(n * SUB, (n + 1) * SUB)
        own = own_ref[:, at].astype(jnp.float32)
        got = got_ref[:, at].astype(jnp.float32)
        sums = jnp.sum(own, axis=0, keepdims=True) + jnp.sum(got, axis=0, keepdims=True)
        means = sums / (2 * rows)
        centred_ref[own_at, at] = (own - means).astype(jnp.bfloat16)
        centred_ref[got_at, at] = (got - means).astype(jnp.bfloat16)

    count = own_ref.shape[1] // SUB
    for n in range(count):
        centre(n)
    for b, (i, j) in enumerate(block_pairs(2 * rows)):
        gram_ref[b] += lax.dot_general(
            centred_ref[i * TILE : (i + 1) * TILE, :],
            centred_ref[j * TILE : (j + 1) * TILE, :],
            (((1,), (1,)), ((), ())),
            preferred_element_type=jnp.float32,
        )


def add_gram(me, log_derivs, got, start, first_block):
    rows, width = got.shape
    total = 2 * rows
    per_core = log_derivs.shape[1] // 2 // WIDE
    return pl.pallas_call(
        gram_kernel,
        grid_spec=pltpu.PrefetchScalarGridSpec(
            num_scalar_prefetch=1,
            grid=(width // WIDE,),
            in_specs=[
                pl.BlockSpec((rows, WIDE), lambda n, me: (0, me[0] * per_core + first_block + n)),
                pl.BlockSpec((rows, WIDE), lambda n, me: (0, n)),
                pl.BlockSpec(start.shape, lambda n, me: (0, 0, 0)),
            ],
            out_specs=[
                pl.BlockSpec((total, WIDE), lambda n, me: (0, n)),
                pl.BlockSpec(start.shape, lambda n, me: (0, 0, 0)),
            ],
        ),
        out_shape=[
            jax.ShapeDtypeStruct((total, width), jnp.bfloat16),
            jax.ShapeDtypeStruct(start.shape, jnp.float32),
        ],
        compiler_params=pltpu.CompilerParams(vmem_limit_bytes=50 * 2**20),
        cost_estimate=pl.CostEstimate(
            flops=int(1.3 * total * total * width), bytes_accessed=8 * rows * width, transcendentals=0
        ),
        name="gram",
    )(me.reshape(1), log_derivs, got, start)


def update_kernel(centred_ref, coeffs_ref, out_ref):
    rows, width = centred_ref.shape
    total = jnp.zeros((16, width), jnp.float32)
    for r in range(0, rows, 16):
        weights = jnp.concatenate([coeffs_ref[r : r + 16, :]] * (width // 128), axis=1)
        total = total + weights * centred_ref[r : r + 16, :].astype(jnp.float32)
    out_ref[...] = jnp.sum(total, axis=0, keepdims=True) * (-1.0 / math.sqrt(rows))


def back_project(coeffs, centred):
    rows, width = centred.shape
    tile = 1024
    return pl.pallas_call(
        update_kernel,
        grid=(width // tile,),
        in_specs=[
            pl.BlockSpec((rows, tile), lambda n: (0, n)),
            pl.BlockSpec((rows, 128), lambda n: (0, 0)),
        ],
        out_specs=pl.BlockSpec((1, tile), lambda n: (0, n)),
        out_shape=jax.ShapeDtypeStruct((1, width), jnp.float32),
        compiler_params=pltpu.CompilerParams(vmem_limit_bytes=40 * 2**20),
        name="update",
    )(centred, coeffs)[0]


HI = lax.Precision.HIGHEST
BLK = 128


def dot_f32(left, right, dims):
    return lax.dot_general(
        left, right, (dims, ((), ())), precision=HI, preferred_element_type=jnp.float32
    )


def factor_diagonal(work, inv_root):
    sub = lax.broadcasted_iota(jnp.int32, (8, BLK), 0)
    lane = lax.broadcasted_iota(jnp.int32, (8, BLK), 1)
    for r in range(0, BLK, 8):
        rows = work[r : r + 8, :]
        upper, side = rows[:, :BLK], rows[:, BLK:]
        cols = [jnp.broadcast_to(upper[:, r + j : r + j + 1], (8, BLK)) for j in range(8)]
        pivots = jnp.ones((8, BLK), jnp.float32)
        for j in range(8):
            recip = 1.0 / jnp.broadcast_to(cols[j][j : j + 1, :], (8, BLK))
            pivots = jnp.where(sub == j, recip, pivots)
            if j == 7:
                break
            ratio = jnp.where(sub > j, cols[j] * recip, 0.0)
            for l in range(j + 1, 8):
                cols[l] = cols[l] - ratio * cols[l][j : j + 1, :]
            upper = upper - ratio * upper[j : j + 1, :]
            side = side - ratio * side[j : j + 1, :]
        inv_root[r : r + 8, :] = side * jnp.sqrt(pivots)
        if r + 8 < BLK:
            scaled = jnp.where(lane >= r + 8, upper * pivots, 0.0)
            change = dot_f32(scaled, jnp.concatenate([upper, side], axis=1), ((0,), (0,)))
            work[r + 8 :, :] = work[r + 8 :, :] - change[r + 8 :, :]


def solve_kernel(gram_ref, energy_ref, out_ref, a, work, inv_roots):
    order = a.shape[0]
    blocks = order // BLK
    for b, (i, j) in enumerate(block_pairs(order)):
        a[i * TILE : (i + 1) * TILE, j * TILE : (j + 1) * TILE] = gram_ref[b] / NP
    eye = jnp.where(
        lax.broadcasted_iota(jnp.int32, (BLK, BLK), 0)
        == lax.broadcasted_iota(jnp.int32, (BLK, BLK), 1),
        1.0,
        0.0,
    )
    diag = jnp.zeros((BLK, BLK), jnp.float32)
    for k in range(blocks):
        s = slice(k * BLK, (k + 1) * BLK)
        diag = diag + eye * a[s, s]
    damping = damp_ratio * (jnp.sum(diag) / order)
    rhs = energy_ref[...]
    rhs = rhs - jnp.sum(rhs, axis=1, keepdims=True) / order
    solved = []
    for k in range(blocks):
        s = slice(k * BLK, (k + 1) * BLK)
        work[:, :BLK] = a[s, s] + damping * eye
        work[:, BLK:] = eye
        factor_diagonal(work, inv_roots.at[k])
        inv_root = inv_roots[k]
        y = dot_f32(rhs[:, :BLK], inv_root, ((1,), (1,)))
        solved.append(y)
        if k + 1 < blocks:
            panel = dot_f32(a[(k + 1) * BLK :, s], inv_root, ((1,), (1,)))
            a[(k + 1) * BLK :, s] = panel
            rhs = rhs[:, BLK:] - dot_f32(y, panel, ((1,), (1,)))
            for c in range(k + 1, blocks):
                t = slice(c * BLK, (c + 1) * BLK)
                a[c * BLK :, t] = a[c * BLK :, t] - dot_f32(
                    panel[(c - k - 1) * BLK :], panel[(c - k - 1) * BLK : (c - k) * BLK], ((1,), (1,))
                )
    below = None
    for k in reversed(range(blocks)):
        z = solved[k]
        if below is not None:
            z = z - dot_f32(below, a[(k + 1) * BLK :, k * BLK : (k + 1) * BLK], ((1,), (0,)))
        x = dot_f32(z, inv_roots[k], ((1,), (0,)))
        below = x if below is None else jnp.concatenate([x, below], axis=1)
    out_ref[...] = below


def solve_system(gram_blocks, energies):
    order = energies.shape[0]
    rows = jnp.broadcast_to(energies[None, :], (8, order))
    out = pl.pallas_call(
        solve_kernel,
        out_shape=jax.ShapeDtypeStruct((8, order), jnp.float32),
        in_specs=[pl.BlockSpec(memory_space=pltpu.VMEM)] * 2,
        out_specs=pl.BlockSpec(memory_space=pltpu.VMEM),
        scratch_shapes=[
            pltpu.VMEM((order, order), jnp.float32),
            pltpu.VMEM((BLK, 2 * BLK), jnp.float32),
            pltpu.VMEM((order // BLK, BLK, BLK), jnp.float32),
        ],
        compiler_params=pltpu.CompilerParams(vmem_limit_bytes=40 * 2**20),
        name="solve",
    )(gram_blocks, rows)
    return out[0]


def local(log_derivs, spin_states, offdiag_energy):
    row_count, width = log_derivs.shape
    cores = lax.axis_size("smp")
    total_rows = row_count * cores
    part = width // cores
    me = lax.axis_index("smp")
    local_energy = lattice_energy(spin_states) + offdiag_energy
    energies = lax.all_gather(local_energy, "smp", axis=0, tiled=True)
    chunks = min(4, part // WIDE)
    chunk = part // chunks
    got = []
    for n in range(chunks):
        theirs = lax.dynamic_slice_in_dim(log_derivs, (1 - me) * part + n * chunk, chunk, 1)
        got.append(lax.ppermute(theirs, "smp", [(0, 1), (1, 0)]))
    gram_blocks = jnp.zeros((len(block_pairs(total_rows)), TILE, TILE), jnp.float32)
    pieces = []
    for n in range(chunks):
        centred, gram_blocks = add_gram(me, log_derivs, got[n], gram_blocks, n * chunk // WIDE)
        pieces.append(centred)
    gram_blocks = lax.psum(gram_blocks, ("par", "smp"))
    coefficients = solve_system(gram_blocks, energies)
    coeffs = jnp.broadcast_to(coefficients[:, None], (total_rows, 128))
    param_update = jnp.concatenate([back_project(coeffs, piece) for piece in pieces])
    return (param_update, coefficients)


def solution(mesh):
    placed = (P(("grp", "smp"), "par"), P(("grp", "smp"), None), P(("grp", "smp")))
    return jax.shard_map(
        local,
        mesh=mesh,
        in_specs=placed,
        out_specs=(P(("grp", "par", "smp")), P("grp")),
        check_vma=False,
    )
```
